256 devices in a mesh: relay: 4 (over x), expert: 16 (over z, core), tensor: 4 (over y).
Axes of the slice: x: 4, y: 4, z: 8, core: 2. Of those that a mesh axis runs over, the one named last changes fastest.
Arguments:
- gate_weight_stack: bfloat16 [16, 4096, 768], P('expert', ('relay', 'tensor')), may hold values from -6 to 6
- up_weight_stack: bfloat16 [16, 4096, 768], P('expert', ('relay', 'tensor')), may hold values from -6 to 6
- down_weight_stack: bfloat16 [16, 4096, 768], P('expert', ('relay', 'tensor')), may hold values from -6 to 6
- adapter_width_factors: bfloat16 [16, 3, 4096, 64], P('expert', None, ('relay', 'tensor')), may hold values from -6 to 6
- adapter_hidden_factors: bfloat16 [16, 3, 64, 768], P('expert', None, None, 'tensor'), may hold values from -0.75 to 0.75
- placement: int32 [16, 16], replicated, may hold values from 0 to 15, as said below
Outputs:
- served: bfloat16 [512, 4, 4, 16, 2304], P('expert', None, 'tensor')
The draws below stay inside these ranges and needn't reach their ends.
Inputs may be any that keep to these rules, and one draw needn't show every extreme that they name: `placement`: each expert sends at most 2 of its 16 slabs to one owner, and some expert sends exactly 2. Each owner receives at most 32 slabs over all experts, and some owner exactly 32.
All inputs are finite; a program needn't handle non-finite values.
Results may differ from the reference program's by a relative error of at most 0.001.
Values may be sent and summed in bfloat16 or wider, within the bound.
No kernel may reach another device: no remote copies, remote signals or barrier semaphores. Data moves between devices by JAX's collectives and lax.ppermute only.
A program may use at most 64 MiB of HBM per device.

```python
import jax
import jax.numpy as jnp
from jax import lax

MODEL_WIDTH = 4096
HIDDEN_WINDOW = 768
ADAPTER_RANK = 64
SLAB = 16
EXPERT_COUNT = 16
ROWS = 256
SLABS = 16
PAIR = 2
CAP = 32
N_RELAY = 4
N_EXPERT = 16
N_TENSOR = 4


def draw_placement(key, part):
    key = jax.random.fold_in(key, 11)
    key_rank, key_owner, key_runs, key_stream, key_shift, key_slabs = jax.random.split(key, 6)
    expert_rank = jax.random.permutation(key_rank, N_EXPERT).astype(jnp.int32)
    owner_order = jax.random.permutation(key_owner, N_EXPERT).astype(jnp.int32)
    run_sizes = jax.random.randint(key_runs, (N_EXPERT - 1,), 1, 3).astype(jnp.int32)
    run_sizes = run_sizes.at[0].set(2)
    run_ends = jnp.cumsum(run_sizes).astype(jnp.int32)
    cycle_size = run_ends[-1]
    hot_count = jnp.clip(CAP - PAIR * expert_rank, 0, PAIR).astype(jnp.int32)
    rest_count = SLABS - hot_count
    stream_order = jax.random.permutation(key_stream, N_EXPERT).astype(jnp.int32)
    rest_in_order = rest_count[stream_order]
    offsets_in_order = (jnp.cumsum(rest_in_order) - rest_in_order).astype(jnp.int32)
    stream_start = jnp.zeros((N_EXPERT,), jnp.int32).at[stream_order].set(offsets_in_order)
    phase = jax.random.randint(key_shift, (), 0, 2 * N_EXPERT).astype(jnp.int32)
    slab_iota = jnp.arange(SLABS, dtype=jnp.int32)
    stream_pos = (stream_start[:, None] + slab_iota[None, :] - hot_count[:, None] + phase) % cycle_size
    cold_index = jnp.sum((stream_pos[:, :, None] >= run_ends[None, None, :]).astype(jnp.int32), axis=-1)
    owner_index = jnp.where(slab_iota[None, :] < hot_count[:, None], 0, 1 + cold_index).astype(jnp.int32)
    slab_keys = jax.random.split(key_slabs, N_EXPERT)
    slab_order = jax.vmap(lambda slab_key: jax.random.permutation(slab_key, SLABS))(slab_keys).astype(jnp.int32)
    shuffled = jnp.take_along_axis(owner_index, slab_order, axis=1)
    return owner_order[shuffled].astype(jnp.int32)


def steps_of(stream_key, dims, cuts, low, top_value):
    factor_of, own = 1.0, jax.random.fold_in(stream_key, 6)
    for dim, parts in cuts:
        draws = jnp.exp(jax.random.uniform(jax.random.fold_in(own, dim), (parts,), jnp.float32, low / len(cuts), top_value / len(cuts)))
        factor_of = factor_of * jnp.repeat(draws, dims[dim] // parts).reshape([-1 if axis == dim else 1 for axis in range(len(dims))])
    return factor_of


def normal_values(key, shape, scale, limit, shards=(), kind=jnp.bfloat16):
    array = scale * jax.random.normal(key, shape, jnp.float32)
    if shards:
        array = array * steps_of(key, shape, shards, -0.22, 0.18)
    return jnp.clip(array, -limit, limit).astype(kind)


def setup_inputs(seed: int = 0) -> dict:
    key_of = jax.random.split(jax.random.key(seed), 7)
    return {
        "gate_weight_stack": normal_values(key_of[0], (EXPERT_COUNT, MODEL_WIDTH, HIDDEN_WINDOW), 1.0, 6.0, ((0, 16), (1, 16))),
        "up_weight_stack": normal_values(key_of[1], (EXPERT_COUNT, MODEL_WIDTH, HIDDEN_WINDOW), 1.0, 6.0, ((0, 16), (1, 16))),
        "down_weight_stack": normal_values(key_of[2], (EXPERT_COUNT, MODEL_WIDTH, HIDDEN_WINDOW), 1.0, 6.0, ((0, 16), (1, 16))),
        "adapter_width_factors": normal_values(key_of[3], (EXPERT_COUNT, 3, MODEL_WIDTH, ADAPTER_RANK), 1.0, 6.0, ((0, 16), (2, 16))),
        "adapter_hidden_factors": normal_values(key_of[4], (EXPERT_COUNT, 3, ADAPTER_RANK, HIDDEN_WINDOW), ADAPTER_RANK ** -0.5, 0.75, ((0, 16), (3, 4))),
        "placement": draw_placement(jax.random.fold_in(key_of[6], 71), 0),
    }


ADAPTER_SCALE = 0.5


def slot_sources(placement):
    flat_table = placement.reshape(-1)
    owner_ids = jnp.arange(N_EXPERT, dtype=jnp.int32)
    owner_hits = flat_table[None, :] == owner_ids[:, None]

    def first_hits(owner_row):
        return jnp.nonzero(owner_row, size=CAP, fill_value=0)[0].astype(jnp.int32)

    position = jax.vmap(first_hits)(owner_hits)
    counts = jnp.sum(owner_hits.astype(jnp.int32), axis=1)
    filled = jnp.arange(CAP, dtype=jnp.int32)[None, :] < counts[:, None]
    return (position // SLABS).reshape(-1), (position % SLABS).reshape(-1), filled.reshape(-1)


def reference(gate_weight_stack, up_weight_stack, down_weight_stack, adapter_width_factors, adapter_hidden_factors, placement):
    expert_ids, slab_ids, filled = slot_sources(placement)
    shard_ids = jnp.arange(N_RELAY * N_TENSOR, dtype=jnp.int32)
    within = jnp.arange(SLAB, dtype=jnp.int32)

    def one_slot(slot_item):
        expert_number, slab_index, is_live = slot_item
        row_numbers = (shard_ids[:, None] * ROWS + slab_index * SLAB + within[None, :]).reshape(-1).astype(jnp.int32)
        gate_weight_rows = jnp.take(gate_weight_stack[expert_number], row_numbers, axis=0).astype(jnp.float32)
        up_weight_rows = jnp.take(up_weight_stack[expert_number], row_numbers, axis=0).astype(jnp.float32)
        down_weight_rows = jnp.take(down_weight_stack[expert_number], row_numbers, axis=0).astype(jnp.float32)
        leftover_rows = jnp.take(adapter_width_factors[expert_number], row_numbers, axis=1).astype(jnp.float32)
        adapter_delta_total = jnp.einsum("qhg,qga->qha", leftover_rows, adapter_hidden_factors[expert_number].astype(jnp.float32))
        merged_gate_weight = gate_weight_rows + ADAPTER_SCALE * adapter_delta_total[0]
        merged_up_weight = up_weight_rows + ADAPTER_SCALE * adapter_delta_total[1]
        merged_down_weight = down_weight_rows + ADAPTER_SCALE * adapter_delta_total[2]
        gate_up = jnp.stack([merged_gate_weight, merged_up_weight], axis=-1).reshape(row_numbers.shape[0], 2 * HIDDEN_WINDOW)
        merged = jnp.concatenate([gate_up, merged_down_weight], axis=1).astype(jnp.bfloat16)
        merged = jnp.where(is_live, merged, jnp.zeros_like(merged))
        return merged.reshape(N_RELAY, N_TENSOR, SLAB, 3 * HIDDEN_WINDOW)

    return lax.map(one_slot, (expert_ids, slab_ids, filled))
```

```python
import functools

import jax
import jax.numpy as jnp
from jax import lax
from jax.experimental import pallas as pl
from jax.experimental.pallas import tpu as pltpu
from jax.sharding import PartitionSpec as P

ADAPTER_SCALE = 0.5
PAIR = 2


def selector(rows, cols, place):
    row = lax.broadcasted_iota(jnp.int32, (rows, cols), 0)
    col = lax.broadcasted_iota(jnp.int32, (rows, cols), 1)
    return jnp.where(col == place(row), 1.0, 0.0).astype(jnp.bfloat16)


def dot(a, b):
    return jnp.dot(a, b, preferred_element_type=jnp.float32)


def dot_t(a, b):
    return lax.dot_general(a, b, (((0,), (0,)), ((), ())), preferred_element_type=jnp.float32)


def merge_kernel(
    index_ref, tensor_ref, gate_ref, up_ref, down_ref, width_ref, v0, v1, v2, v3,
    self_ref, keep_ref, swap_ref, mixed_ref, plain_ref, merged_ref,
):
    slabs = index_ref.shape[0]
    rows, hidden = gate_ref.shape
    slab_rows = rows // slabs
    rank = width_ref.shape[1]
    part = v0.shape[2]
    me = tensor_ref[0]
    even = selector(part, 2 * part, lambda row: 2 * row)
    odd = selector(part, 2 * part, lambda row: 2 * row + 1)
    plain_ref[...] = jnp.zeros_like(plain_ref)
    for j, v in enumerate((v0, v1, v2, v3)):
        home = lax.rem(me - j + 4, 4)
        cols = pl.ds(pl.multiple_of(home * (2 * part), 128), 2 * part)
        mixed_ref[:rank, cols] = dot(v[0], even).astype(jnp.bfloat16)
        mixed_ref[rank:, cols] = dot(v[1], odd).astype(jnp.bfloat16)
        shift = lax.rem(home, 2) * part
        pair_cols = pl.ds(pl.multiple_of(lax.div(home, 2) * (2 * part), 128), 2 * part)
        plain_ref[:, pair_cols] += dot(v[2], selector(part, 2 * part, lambda row: row + shift))
    half = 128
    spread = selector(
        2 * half, 2 * half, lambda row: jnp.where(row < half, 2 * row, 2 * (row - half) + 1)
    )
    both = width_ref[0:2].reshape(2 * rank, rows)
    for block in range(hidden // half):
        src = slice(block * half, (block + 1) * half)
        dst = slice(2 * block * half, 2 * (block + 1) * half)
        weight = dot(jnp.concatenate([gate_ref[:, src], up_ref[:, src]], axis=1), spread)
        delta = dot_t(both, mixed_ref[:, dst])
        merged_ref[:, dst] = (weight + ADAPTER_SCALE * delta).astype(jnp.bfloat16)
    delta = dot_t(width_ref[2], plain_ref[...].astype(jnp.bfloat16))
    merged_ref[:, 2 * hidden :] = (
        down_ref[...].astype(jnp.float32) + ADAPTER_SCALE * delta
    ).astype(jnp.bfloat16)
    bucket = swap_ref.shape[0]
    for k in range(slabs):
        index = index_ref[k]
        block = slice(k * slab_rows, (k + 1) * slab_rows)

        @pl.when(index < PAIR)
        def _():
            self_ref[index] = merged_ref[block, :]

        @pl.when((index >= PAIR) & (index < bucket))
        def _():
            keep_ref[index - PAIR] = merged_ref[block, :]

        @pl.when(index >= bucket)
        def _():
            swap_ref[index - bucket] = merged_ref[block, :]


def merge(index, tensor, gate, up, down, width, parts):
    rows, hidden = gate.shape
    rank = width.shape[1]
    slab_rows = rows // index.shape[0]
    wide = 3 * hidden
    smem = pl.BlockSpec(memory_space=pltpu.SMEM)
    vmem = pl.BlockSpec(memory_space=pltpu.VMEM)

    def slots(n):
        return jax.ShapeDtypeStruct((n, slab_rows, wide), jnp.bfloat16)

    return pl.pallas_call(
        merge_kernel,
        out_shape=[slots(PAIR), slots(16 - PAIR), slots(16)],
        in_specs=[smem, smem] + [vmem] * 8,
        out_specs=[vmem] * 3,
        scratch_shapes=[
            pltpu.VMEM((2 * rank, 2 * hidden), jnp.bfloat16),
            pltpu.VMEM((rank, hidden), jnp.float32),
            pltpu.VMEM((rows, wide), jnp.bfloat16),
        ],
        compiler_params=pltpu.CompilerParams(vmem_limit_bytes=24 << 20),
        cost_estimate=pl.CostEstimate(
            flops=2 * rows * wide * 384, bytes_accessed=4_000_000, transcendentals=0
        ),
    )(index, tensor, gate, up, down, width, *parts)


def assemble_kernel(plan, dest_ref, count_ref, relay_ref, *refs):
    bufs, (out_ref, zero_ref, sem) = refs[:-3], refs[-3:]
    groups = out_ref.shape[1]
    zero_ref[...] = jnp.zeros_like(zero_ref)
    for slot, pieces in enumerate(plan):
        dest = dest_ref[slot]

        @pl.when(dest >= 0)
        def _():
            for which, row, shift in pieces:
                group = lax.rem(relay_ref[0] + shift, groups)
                pltpu.make_async_copy(
                    bufs[which].at[row], out_ref.at[dest, group, 0], sem
                ).start()

    @pl.loop(count_ref[0], out_ref.shape[0])
    def _(slot):
        pltpu.make_async_copy(zero_ref, out_ref.at[slot], sem).start()

    pltpu.make_async_copy(out_ref, out_ref, sem).wait()


def assemble(plan, dest, count, relay, bufs, out_shape):
    smem = pl.BlockSpec(memory_space=pltpu.SMEM)
    anywhere = pl.BlockSpec(memory_space=pl.ANY)
    return pl.pallas_call(
        functools.partial(assemble_kernel, plan),
        out_shape=jax.ShapeDtypeStruct(out_shape, jnp.bfloat16),
        in_specs=[smem] * 3 + [anywhere] * len(bufs),
        out_specs=anywhere,
        scratch_shapes=[pltpu.VMEM(out_shape[1:], jnp.bfloat16), pltpu.SemaphoreType.DMA],
        cost_estimate=pl.CostEstimate(flops=0, bytes_accessed=18_000_000, transcendentals=0),
    )(dest, count, relay, *bufs)


def shift(value, axis, by):
    size = lax.axis_size(axis)
    return lax.ppermute(value, axis, [(i, (i + by) % size) for i in range(size)])


def body(gate, up, down, width, hidden, placement):
    owners = lax.axis_size("expert")
    chips = owners // 2
    slabs = placement.shape[1]
    me = lax.axis_index("expert").astype(jnp.int32)
    targets = lax.dynamic_index_in_dim(placement, me, 0, keepdims=False)
    iota = jnp.arange(slabs, dtype=jnp.int32)
    order = jnp.sum(
        ((targets[None, :] == targets[:, None]) & (iota[None, :] < iota[:, None])).astype(jnp.int32),
        axis=1,
    )
    offset = (targets // 2 - me // 2) % chips
    index = ((targets ^ me) & 1) * (PAIR * chips) + offset * PAIR + order
    hits = jnp.sum((placement == me).astype(jnp.int32), axis=1)
    before = jnp.sum(jnp.where(iota[None, :] < iota[:, None], hits[None, :], 0), axis=1)
    total = jnp.sum(hits)
    pair = jnp.arange(PAIR, dtype=jnp.int32)
    table = jnp.where(pair[None, :] < hits[:, None], before[:, None] + pair[None, :], -1)

    parts = [hidden[0]] + [shift(hidden[0], "tensor", k) for k in (1, 2, 3)]
    own, keep, swap = merge(
        index,
        lax.axis_index("tensor").astype(jnp.int32)[None],
        gate[0], up[0], down[0],
        jnp.swapaxes(width[0], 1, 2),
        parts,
    )
    mate = [(i, i ^ 1) for i in range(owners)]
    got = lax.ppermute(swap, "expert", mate)

    def send(d):
        rows = slice(PAIR * (d - 1), PAIR * d)
        message = jnp.concatenate([keep[rows], got[PAIR * d : PAIR * (d + 1)]], axis=0)
        return shift(message, "expert", 2 * d)

    def pair_of(d):
        return [send(d), send(chips - d)]

    steps = [
        ([0], [own]),
        ([-1], [got[:PAIR]]),
        ([1, chips - 1], None),
        ([2, chips - 2], None),
        ([3, chips - 3], None),
        ([4], None),
        ([], []),
    ]
    bufs, plan, sources = [], [], []
    forward_right = forward_left = None
    pending = []
    for names, items in steps:
        items = [send(d) for d in names] if items is None else items
        count = sum(item.shape[0] for item in items)
        right = items + ([] if forward_right is None else [forward_right])
        left = items + ([] if forward_left is None else [forward_left])
        right = right[0] if len(right) == 1 else jnp.concatenate(right, axis=0)
        left = left[0] if len(left) == 1 else jnp.concatenate(left, axis=0)
        from_left = shift(right, "relay", 1)
        from_right = shift(left, "relay", -1)
        at_left, at_right = len(bufs), len(bufs) + 1
        bufs += [from_left, from_right]
        for j, entry in enumerate(pending):
            half = len(pending) // 2
            piece = (at_left, count + j, 2) if j < half else (at_right, count + j - half, 2)
            plan[entry].append(piece)
        pending = []
        row = 0
        for name, item in zip(names, items):
            bufs.append(item)
            for j in range(item.shape[0]):
                core = j // PAIR
                source = me ^ 1 if name < 0 else ((me - 2 * name) % owners) ^ core
                if j % PAIR == 0:
                    sources.append(source)
                pending.append(len(plan))
                plan.append([(len(bufs) - 1, j, 0), (at_left, row, 3), (at_right, row, 1)])
                row += 1
        if count:
            forward_right = from_left[: count // 2]
            forward_left = from_right[count // 2 : count]
    sources = jnp.stack(sources)
    dest = jnp.sum(
        jnp.where(sources[:, None, None] == iota[None, :, None], table[None], 0), axis=1
    ).reshape(-1)
    slab_rows, wide = own.shape[1:]
    return assemble(
        tuple(tuple(p) for p in plan),
        dest,
        total[None],
        lax.axis_index("relay").astype(jnp.int32)[None],
        bufs,
        (owners * PAIR, lax.axis_size("relay"), 1, slab_rows, wide),
    )


def solution(mesh):
    return jax.shard_map(
        body,
        mesh=mesh,
        in_specs=(
            P("expert", ("relay", "tensor"), None),
            P("expert", ("relay", "tensor"), None),
            P("expert", ("relay", "tensor"), None),
            P("expert", None, ("relay", "tensor"), None),
            P("expert", None, None, "tensor"),
            P(),
        ),
        out_specs=P("expert", None, "tensor", None, None),
        check_vma=False,
    )
```

```python
import functools

import jax
import jax.numpy as jnp
from jax import lax
from jax.experimental import pallas as pl
from jax.experimental.pallas import tpu as pltpu
from jax.sharding import PartitionSpec as P

ADAPTER_SCALE = 0.5
PAIR = 2


def selector(rows, cols, place):
    row = lax.broadcasted_iota(jnp.int32, (rows, cols), 0)
    col = lax.broadcasted_iota(jnp.int32, (rows, cols), 1)
    return jnp.where(col == place(row), 1.0, 0.0).astype(jnp.bfloat16)


def dot(a, b):
    return jnp.dot(a, b, preferred_element_type=jnp.float32)


def dot_t(a, b):
    return lax.dot_general(a, b, (((0,), (0,)), ((), ())), preferred_element_type=jnp.float32)


def merge_kernel(
    index_ref, tensor_ref, gate_hbm, up_hbm, down_hbm, width_hbm, v0, v1, v2, v3,
    self_ref, keep_ref, swap_ref, mixed_ref, plain_ref, merged_ref,
    gate_ref, up_ref, down_ref, width_ref, parts_ref, sems,
):
    parts = [parts_ref.at[j] for j in range(4)]
    loads = [
        pltpu.make_async_copy(src, dst, sems.at[j])
        for j, (src, dst) in enumerate(
            zip(
                (v0, v1, v2, v3, gate_hbm, up_hbm, width_hbm, down_hbm),
                (*parts, gate_ref, up_ref, width_ref, down_ref),
            )
        )
    ]
    for load in loads:
        load.start()
    slabs = index_ref.shape[0]
    rows, hidden = gate_ref.shape
    slab_rows = rows // slabs
    rank = width_ref.shape[1]
    part = parts_ref.shape[3]
    me = tensor_ref[0]
    even = selector(part, 2 * part, lambda row: 2 * row)
    odd = selector(part, 2 * part, lambda row: 2 * row + 1)
    plain_ref[...] = jnp.zeros_like(plain_ref)
    for j, v in enumerate(parts):
        loads[j].wait()
        home = lax.rem(me - j + 4, 4)
        cols = pl.ds(pl.multiple_of(home * (2 * part), 128), 2 * part)
        mixed_ref[:rank, cols] = dot(v[0], even).astype(jnp.bfloat16)
        mixed_ref[rank:, cols] = dot(v[1], odd).astype(jnp.bfloat16)
        shift = lax.rem(home, 2) * part
        pair_cols = pl.ds(pl.multiple_of(lax.div(home, 2) * (2 * part), 128), 2 * part)
        plain_ref[:, pair_cols] += dot(v[2], selector(part, 2 * part, lambda row: row + shift))
    half = 128
    spread = selector(
        2 * half, 2 * half, lambda row: jnp.where(row < half, 2 * row, 2 * (row - half) + 1)
    )
    for load in loads[4:]:
        load.wait()
    both = width_ref[0:2].reshape(2 * rank, rows)
    for block in range(hidden // half):
        src = slice(block * half, (block + 1) * half)
        dst = slice(2 * block * half, 2 * (block + 1) * half)
        weight = dot(jnp.concatenate([gate_ref[:, src], up_ref[:, src]], axis=1), spread)
        delta = dot_t(both, mixed_ref[:, dst])
        merged_ref[:, dst] = (weight + ADAPTER_SCALE * delta).astype(jnp.bfloat16)
    delta = dot_t(width_ref[2], plain_ref[...].astype(jnp.bfloat16))
    merged_ref[:, 2 * hidden :] = (
        down_ref[...].astype(jnp.float32) + ADAPTER_SCALE * delta
    ).astype(jnp.bfloat16)
    bucket = swap_ref.shape[0]
    for k in range(slabs):
        index = index_ref[k]
        block = slice(k * slab_rows, (k + 1) * slab_rows)

        @pl.when(index < PAIR)
        def _():
            self_ref[index] = merged_ref[block, :]

        @pl.when((index >= PAIR) & (index < bucket))
        def _():
            keep_ref[index - PAIR] = merged_ref[block, :]

        @pl.when(index >= bucket)
        def _():
            swap_ref[index - bucket] = merged_ref[block, :]


def merge(index, tensor, gate, up, down, width, parts):
    rows, hidden = gate.shape
    rank = width.shape[1]
    slab_rows = rows // index.shape[0]
    wide = 3 * hidden
    smem = pl.BlockSpec(memory_space=pltpu.SMEM)
    vmem = pl.BlockSpec(memory_space=pltpu.VMEM)

    def slots(n):
        return jax.ShapeDtypeStruct((n, slab_rows, wide), jnp.bfloat16)

    return pl.pallas_call(
        merge_kernel,
        out_shape=[slots(PAIR), slots(16 - PAIR), slots(16)],
        in_specs=[smem, smem] + [pl.BlockSpec(memory_space=pl.ANY)] * 8,
        out_specs=[vmem] * 3,
        scratch_shapes=[
            pltpu.VMEM((2 * rank, 2 * hidden), jnp.bfloat16),
            pltpu.VMEM((rank, hidden), jnp.float32),
            pltpu.VMEM((rows, wide), jnp.bfloat16),
            pltpu.VMEM((rows, hidden), jnp.bfloat16),
            pltpu.VMEM((rows, hidden), jnp.bfloat16),
            pltpu.VMEM((rows, hidden), jnp.bfloat16),
            pltpu.VMEM(width.shape, jnp.bfloat16),
            pltpu.VMEM((4, *parts[0].shape), jnp.bfloat16),
            pltpu.SemaphoreType.DMA((8,)),
        ],
        cost_estimate=pl.CostEstimate(
            flops=2 * rows * wide * 384, bytes_accessed=4_000_000, transcendentals=0
        ),
    )(index, tensor, gate, up, down, width, *parts)


def place_kernel(pieces, first, dest_ref, count_ref, relay_ref, *refs):
    if first:
        bufs, (out_ref, sems, zero_ref, zero_sems) = refs[:-4], refs[-4:]
    else:
        bufs, (_, out_ref, sems) = refs[:-3], refs[-3:]
    groups = out_ref.shape[1]

    def copy(number):
        which, row, entry, shift = pieces[number]
        group = lax.rem(relay_ref[0] + shift, groups)
        dest = jnp.maximum(dest_ref[entry], 0)
        return pltpu.make_async_copy(
            bufs[which].at[row], out_ref.at[dest, group, 0], sems.at[number]
        )

    def blank(slot):
        return pltpu.make_async_copy(zero_ref, out_ref.at[slot], zero_sems.at[slot])

    for number, piece in enumerate(pieces):

        @pl.when(dest_ref[piece[2]] >= 0)
        def _():
            copy(number).start()

    if first:
        zero_ref[...] = jnp.zeros_like(zero_ref)

        @pl.loop(count_ref[0], out_ref.shape[0])
        def _(slot):
            blank(slot).start()

        @pl.loop(count_ref[0], out_ref.shape[0])
        def _(slot):
            blank(slot).wait()

    for number, piece in enumerate(pieces):

        @pl.when(dest_ref[piece[2]] >= 0)
        def _():
            copy(number).wait()


def place(out, pieces, dest, count, relay, bufs, out_shape):
    smem = pl.BlockSpec(memory_space=pltpu.SMEM)
    vmem = pl.BlockSpec(memory_space=pltpu.VMEM)
    anywhere = pl.BlockSpec(memory_space=pl.ANY)
    first = out is None
    scratch = [pltpu.SemaphoreType.DMA((len(pieces),))]
    if first:
        scratch += [
            pltpu.VMEM(out_shape[1:], jnp.bfloat16),
            pltpu.SemaphoreType.DMA((out_shape[0],)),
        ]
    return pl.pallas_call(
        functools.partial(place_kernel, pieces, first),
        out_shape=jax.ShapeDtypeStruct(out_shape, jnp.bfloat16),
        in_specs=[smem] * 3 + [vmem] * len(bufs) + ([] if first else [anywhere]),
        out_specs=anywhere,
        scratch_shapes=scratch,
        input_output_aliases={} if first else {3 + len(bufs): 0},
        cost_estimate=pl.CostEstimate(
            flops=0, bytes_accessed=len(pieces) * 73728, transcendentals=0
        ),
    )(dest, count, relay, *bufs, *([] if first else [out]))


def shift(value, axis, by):
    size = lax.axis_size(axis)
    return lax.ppermute(value, axis, [(i, (i + by) % size) for i in range(size)])


def body(gate, up, down, width, hidden, placement):
    owners = lax.axis_size("expert")
    chips = owners // 2
    slabs = placement.shape[1]
    me = lax.axis_index("expert").astype(jnp.int32)
    targets = lax.dynamic_index_in_dim(placement, me, 0, keepdims=False)
    iota = jnp.arange(slabs, dtype=jnp.int32)
    order = jnp.sum(
        ((targets[None, :] == targets[:, None]) & (iota[None, :] < iota[:, None])).astype(jnp.int32),
        axis=1,
    )
    offset = (targets // 2 - me // 2) % chips
    index = ((targets ^ me) & 1) * (PAIR * chips) + offset * PAIR + order
    hits = jnp.sum((placement == me).astype(jnp.int32), axis=1)
    before = jnp.sum(jnp.where(iota[None, :] < iota[:, None], hits[None, :], 0), axis=1)
    total = jnp.sum(hits)
    pair = jnp.arange(PAIR, dtype=jnp.int32)
    table = jnp.where(pair[None, :] < hits[:, None], before[:, None] + pair[None, :], -1)

    parts = [hidden[0]] + [shift(hidden[0], "tensor", k) for k in (1, 2, 3)]
    own, keep, swap = merge(
        index,
        lax.axis_index("tensor").astype(jnp.int32)[None],
        gate[0], up[0], down[0],
        jnp.swapaxes(width[0], 1, 2),
        parts,
    )
    mate = [(i, i ^ 1) for i in range(owners)]
    got = lax.ppermute(swap, "expert", mate)

    def send(d):
        rows = slice(PAIR * (d - 1), PAIR * d)
        message = jnp.concatenate([keep[rows], got[PAIR * d : PAIR * (d + 1)]], axis=0)
        return shift(message, "expert", 2 * d)

    def pair_of(d):
        return [send(d), send(chips - d)]

    near = jnp.concatenate([own, got[:PAIR]], axis=0)
    steps = [
        ([0], [near], False, False),
        ([1, chips - 1], None, False, False),
        ([2, chips - 2], None, False, False),
        ([3, chips - 3], None, True, False),
        ([4], None, True, True),
        ([], [], False, True),
    ]
    sources = jnp.stack(
        [((me - 2 * d) % owners) ^ core for names, *_ in steps for d in names for core in (0, 1)]
    )
    dest = jnp.sum(
        jnp.where(sources[:, None, None] == iota[None, :, None], table[None], 0), axis=1
    ).reshape(-1)
    relay = lax.axis_index("relay").astype(jnp.int32)[None]
    slab_rows, wide = own.shape[1:]
    out_shape = (owners * PAIR, lax.axis_size("relay"), 1, slab_rows, wide)
    def ring(parts, by):
        arrived = []
        for part in parts:
            message = part[0] if len(part) == 1 else jnp.concatenate(part, axis=0)
            bufs.append(shift(message, "relay", by))
            arrived += [(len(bufs) - 1, row) for row in range(message.shape[0])]
        return arrived

    def messages(front, back, forward, split):
        rest = back + forward
        if split:
            return [front] + ([rest] if rest else [])
        return [front + rest]

    out, bufs, pieces = None, [], []
    forward_right, forward_left, entry, earlier = [], [], 0, []
    for names, items, split, flush in steps:
        items = [send(d) for d in names] if items is None else items
        first, last = items[:1], items[1:]
        from_left = ring(messages(first, last, forward_right, split), 1)
        from_right = ring(
            messages(last, first, forward_left, split)
            if len(items) == 2
            else messages(first, last, forward_left, split),
            -1,
        )
        held = []
        for item in items:
            bufs.append(item)
            held.append([(len(bufs) - 1, row) for row in range(item.shape[0])])
        count = sum(len(rows) for rows in held)
        order = held[0] + (held[1] if len(held) == 2 else []) if held else []
        turned = held[1] + held[0] if len(held) == 2 else order
        half = len(earlier) // 2
        pieces += [(*from_left[count + j], earlier[j], 2) for j in range(half)]
        pieces += [(*from_right[count + j], earlier[half + j], 2) for j in range(half)]
        base = entry
        where = {slot: base + j for j, slot in enumerate(order)}
        for j in range(count):
            pieces += [
                (*order[j], base + j, 0),
                (*from_left[j], where[order[j]], 3),
                (*from_right[j], where[turned[j]], 1),
            ]
        earlier = [base + j for j in range(count)]
        entry += count
        half = count // 2
        forward_right = forward_left = []
        if count:
            left_buf, right_buf = bufs[from_left[0][0]], bufs[from_right[0][0]]
            forward_right = [left_buf if left_buf.shape[0] == half else left_buf[:half]]
            if len(items) == 2:
                forward_left = [right_buf if right_buf.shape[0] == half else right_buf[:half]]
            else:
                forward_left = [right_buf[half:count]]
        if flush:
            out = place(out, pieces, dest, total[None], relay, bufs, out_shape)
            bufs, pieces = [], []
    return out


def solution(mesh):
    return jax.shard_map(
        body,
        mesh=mesh,
        in_specs=(
            P("expert", ("relay", "tensor"), None),
            P("expert", ("relay", "tensor"), None),
            P("expert", ("relay", "tensor"), None),
            P("expert", None, ("relay", "tensor"), None),
            P("expert", None, None, "tensor"),
            P(),
        ),
        out_specs=P("expert", None, "tensor", None, None),
        check_vma=False,
    )
```

```python
import functools

import jax
import jax.numpy as jnp
from jax import lax
from jax.experimental import pallas as pl
from jax.experimental.pallas import tpu as pltpu
from jax.sharding import PartitionSpec as P

ADAPTER_SCALE = 0.5
PAIR = 2


def selector(rows, cols, place):
    row = lax.broadcasted_iota(jnp.int32, (rows, cols), 0)
    col = lax.broadcasted_iota(jnp.int32, (rows, cols), 1)
    return jnp.where(col == place(row), 1.0, 0.0).astype(jnp.bfloat16)


def dot(a, b):
    return jnp.dot(a, b, preferred_element_type=jnp.float32)


def dot_t(a, b):
    return lax.dot_general(a, b, (((0,), (0,)), ((), ())), preferred_element_type=jnp.float32)


def weave_kernel(gate_hbm, up_hbm, down_hbm, woven_ref, gate_ref, up_ref, sems):
    rows, hidden = gate_ref.shape
    loads = [
        pltpu.make_async_copy(gate_hbm, gate_ref, sems.at[0]),
        pltpu.make_async_copy(up_hbm, up_ref, sems.at[1]),
        pltpu.make_async_copy(down_hbm, woven_ref.at[:, pl.ds(2 * hidden, hidden)], sems.at[2]),
    ]
    for load in loads:
        load.start()
    half = 128
    spread = selector(
        2 * half, 2 * half, lambda row: jnp.where(row < half, 2 * row, 2 * (row - half) + 1)
    )
    loads[0].wait()
    loads[1].wait()
    for block in range(hidden // half):
        src = slice(block * half, (block + 1) * half)
        dst = slice(2 * block * half, 2 * (block + 1) * half)
        both = jnp.concatenate([gate_ref[:, src], up_ref[:, src]], axis=1)
        woven_ref[:, dst] = dot(both, spread).astype(jnp.bfloat16)
    loads[2].wait()


def weave(gate, up, down):
    rows, hidden = gate.shape
    return pl.pallas_call(
        weave_kernel,
        out_shape=jax.ShapeDtypeStruct((rows, 3 * hidden), jnp.bfloat16),
        in_specs=[pl.BlockSpec(memory_space=pl.ANY)] * 3,
        out_specs=pl.BlockSpec(memory_space=pltpu.VMEM),
        scratch_shapes=[
            pltpu.VMEM((rows, hidden), jnp.bfloat16),
            pltpu.VMEM((rows, hidden), jnp.bfloat16),
            pltpu.SemaphoreType.DMA((3,)),
        ],
        compiler_params=pltpu.CompilerParams(vmem_limit_bytes=8 << 20),
        cost_estimate=pl.CostEstimate(
            flops=2 * rows * hidden * 512, bytes_accessed=2_400_000, transcendentals=0
        ),
    )(gate, up, down)


def merge_kernel(
    index_ref, tensor_ref, woven_ref, width_hbm, own_hbm, v1, v2, v3,
    self_ref, keep_ref, swap_ref, mixed_ref, plain_ref, merged_ref, width_ref, own_ref, sems,
):
    loads = [
        pltpu.make_async_copy(own_hbm, own_ref, sems.at[0]),
        pltpu.make_async_copy(width_hbm, width_ref, sems.at[1]),
    ]
    for load in loads:
        load.start()
    slabs = index_ref.shape[0]
    rows, wide = woven_ref.shape
    hidden = wide // 3
    slab_rows = rows // slabs
    rank = width_ref.shape[1]
    part = own_ref.shape[2]
    me = tensor_ref[0]
    even = selector(part, 2 * part, lambda row: 2 * row)
    odd = selector(part, 2 * part, lambda row: 2 * row + 1)
    plain_ref[...] = jnp.zeros_like(plain_ref)
    for j, v in ((1, v1), (2, v2), (3, v3), (0, own_ref)):
        if j == 0:
            loads[0].wait()
        home = lax.rem(me - j + 4, 4)
        cols = pl.ds(pl.multiple_of(home * (2 * part), 128), 2 * part)
        mixed_ref[:rank, cols] = dot(v[0], even).astype(jnp.bfloat16)
        mixed_ref[rank:, cols] = dot(v[1], odd).astype(jnp.bfloat16)
        shift = lax.rem(home, 2) * part
        pair_cols = pl.ds(pl.multiple_of(lax.div(home, 2) * (2 * part), 128), 2 * part)
        plain_ref[:, pair_cols] += dot(v[2], selector(part, 2 * part, lambda row: row + shift))
    loads[1].wait()
    both = width_ref[0:2].reshape(2 * rank, rows)
    for block in range(2 * hidden // 256):
        dst = slice(block * 256, (block + 1) * 256)
        delta = dot_t(both, mixed_ref[:, dst])
        merged_ref[:, dst] = (
            woven_ref[:, dst].astype(jnp.float32) + ADAPTER_SCALE * delta
        ).astype(jnp.bfloat16)
    delta = dot_t(width_ref[2], plain_ref[...].astype(jnp.bfloat16))
    merged_ref[:, 2 * hidden :] = (
        woven_ref[:, 2 * hidden :].astype(jnp.float32) + ADAPTER_SCALE * delta
    ).astype(jnp.bfloat16)
    bucket = swap_ref.shape[0]
    for k in range(slabs):
        index = index_ref[k]
        block = slice(k * slab_rows, (k + 1) * slab_rows)

        @pl.when(index < PAIR)
        def _():
            self_ref[index] = merged_ref[block, :]

        @pl.when((index >= PAIR) & (index < bucket))
        def _():
            keep_ref[index - PAIR] = merged_ref[block, :]

        @pl.when(index >= bucket)
        def _():
            swap_ref[index - bucket] = merged_ref[block, :]


def merge(index, tensor, woven, width, parts):
    rows, wide = woven.shape
    rank = width.shape[1]
    slab_rows = rows // index.shape[0]
    smem = pl.BlockSpec(memory_space=pltpu.SMEM)
    vmem = pl.BlockSpec(memory_space=pltpu.VMEM)

    def slots(n):
        return jax.ShapeDtypeStruct((n, slab_rows, wide), jnp.bfloat16)

    return pl.pallas_call(
        merge_kernel,
        out_shape=[slots(PAIR), slots(16 - PAIR), slots(16)],
        in_specs=[smem, smem, vmem] + [pl.BlockSpec(memory_space=pl.ANY)] * 2 + [vmem] * 3,
        out_specs=[vmem] * 3,
        scratch_shapes=[
            pltpu.VMEM((2 * rank, 2 * wide // 3), jnp.bfloat16),
            pltpu.VMEM((rank, wide // 3), jnp.float32),
            pltpu.VMEM((rows, wide), jnp.bfloat16),
            pltpu.VMEM(width.shape, jnp.bfloat16),
            pltpu.VMEM(parts[0].shape, jnp.bfloat16),
            pltpu.SemaphoreType.DMA((2,)),
        ],
        compiler_params=pltpu.CompilerParams(vmem_limit_bytes=12 << 20),
        cost_estimate=pl.CostEstimate(
            flops=2 * rows * wide * 128, bytes_accessed=4_000_000, transcendentals=0
        ),
    )(index, tensor, woven, width, *parts)


def place_kernel(pieces, count, first, dest_ref, count_ref, relay_ref, *refs):
    bufs, refs = refs[:count], refs[count if first else count + 1 :]
    out_ref, refs = refs[0], refs[1:]
    held, refs = refs[:count], refs[count:]
    load_sems, sems = refs[:2]
    groups = out_ref.shape[1]
    loads = [pltpu.make_async_copy(bufs[j], held[j], load_sems.at[j]) for j in range(count)]
    for load in loads:
        load.start()

    def copy(number):
        which, row, entry, shift = pieces[number]
        group = lax.rem(relay_ref[0] + shift, groups)
        dest = jnp.maximum(dest_ref[entry], 0)
        return pltpu.make_async_copy(
            held[which].at[row], out_ref.at[dest, group, 0], sems.at[number]
        )

    if first:
        zero_ref, zero_sems = refs[2:]

        def blank(slot):
            return pltpu.make_async_copy(zero_ref, out_ref.at[slot], zero_sems.at[slot])

        zero_ref[...] = jnp.zeros_like(zero_ref)

        @pl.loop(count_ref[0], out_ref.shape[0])
        def _(slot):
            blank(slot).start()

    ready = set()
    for number, piece in enumerate(pieces):
        if piece[0] not in ready:
            ready.add(piece[0])
            loads[piece[0]].wait()

        @pl.when(dest_ref[piece[2]] >= 0)
        def _():
            copy(number).start()

    if first:

        @pl.loop(count_ref[0], out_ref.shape[0])
        def _(slot):
            blank(slot).wait()

    for number, piece in enumerate(pieces):

        @pl.when(dest_ref[piece[2]] >= 0)
        def _():
            copy(number).wait()


def place(out, pieces, dest, total, relay, bufs, out_shape):
    smem = pl.BlockSpec(memory_space=pltpu.SMEM)
    anywhere = pl.BlockSpec(memory_space=pl.ANY)
    first = out is None
    count = len(bufs)
    pieces = sorted(pieces)
    scratch = [pltpu.VMEM(buf.shape, jnp.bfloat16) for buf in bufs]
    scratch += [pltpu.SemaphoreType.DMA((count,)), pltpu.SemaphoreType.DMA((len(pieces),))]
    if first:
        scratch += [
            pltpu.VMEM(out_shape[1:], jnp.bfloat16),
            pltpu.SemaphoreType.DMA((out_shape[0],)),
        ]
    return pl.pallas_call(
        functools.partial(place_kernel, pieces, count, first),
        out_shape=jax.ShapeDtypeStruct(out_shape, jnp.bfloat16),
        in_specs=[smem] * 3 + [anywhere] * (count if first else count + 1),
        out_specs=anywhere,
        scratch_shapes=scratch,
        input_output_aliases={} if first else {3 + count: 0},
        cost_estimate=pl.CostEstimate(
            flops=0, bytes_accessed=2 * len(pieces) * 73728, transcendentals=0
        ),
    )(dest, total, relay, *bufs, *([] if first else [out]))


def shift(value, axis, by):
    size = lax.axis_size(axis)
    return lax.ppermute(value, axis, [(i, (i + by) % size) for i in range(size)])


def body(gate, up, down, width, hidden, placement):
    owners = lax.axis_size("expert")
    chips = owners // 2
    slabs = placement.shape[1]
    me = lax.axis_index("expert").astype(jnp.int32)
    targets = lax.dynamic_index_in_dim(placement, me, 0, keepdims=False)
    iota = jnp.arange(slabs, dtype=jnp.int32)
    order = jnp.sum(
        ((targets[None, :] == targets[:, None]) & (iota[None, :] < iota[:, None])).astype(jnp.int32),
        axis=1,
    )
    offset = (targets // 2 - me // 2) % chips
    index = ((targets ^ me) & 1) * (PAIR * chips) + offset * PAIR + order
    hits = jnp.sum((placement == me).astype(jnp.int32), axis=1)
    before = jnp.sum(jnp.where(iota[None, :] < iota[:, None], hits[None, :], 0), axis=1)
    total = jnp.sum(hits)
    pair = jnp.arange(PAIR, dtype=jnp.int32)
    table = jnp.where(pair[None, :] < hits[:, None], before[:, None] + pair[None, :], -1)

    parts = [hidden[0]] + [shift(hidden[0], "tensor", k) for k in (1, 2, 3)]
    own, keep, swap = merge(
        index,
        lax.axis_index("tensor").astype(jnp.int32)[None],
        weave(gate[0], up[0], down[0]),
        jnp.swapaxes(width[0], 1, 2),
        parts,
    )
    mate = [(i, i ^ 1) for i in range(owners)]
    got = lax.ppermute(swap, "expert", mate)

    def send(d):
        rows = slice(PAIR * (d - 1), PAIR * d)
        message = jnp.concatenate([keep[rows], got[PAIR * d : PAIR * (d + 1)]], axis=0)
        return shift(message, "expert", 2 * d)

    def pair_of(d):
        return [send(d), send(chips - d)]

    near = jnp.concatenate([own, got[:PAIR]], axis=0)
    steps = [
        ([0], [near], False, False),
        ([1, chips - 1], None, False, False),
        ([2, chips - 2], None, False, True),
        ([3, chips - 3], None, False, False),
        ([4], None, True, True),
    ]
    sources = jnp.stack(
        [((me - 2 * d) % owners) ^ core for names, *_ in steps for d in names for core in (0, 1)]
    )
    dest = jnp.sum(
        jnp.where(sources[:, None, None] == iota[None, :, None], table[None], 0), axis=1
    ).reshape(-1)
    relay = lax.axis_index("relay").astype(jnp.int32)[None]
    slab_rows, wide = own.shape[1:]
    out_shape = (owners * PAIR, lax.axis_size("relay"), 1, slab_rows, wide)
    def ring(parts, by):
        arrived = []
        for part in parts:
            message = part[0] if len(part) == 1 else jnp.concatenate(part, axis=0)
            bufs.append(shift(message, "relay", by))
            arrived += [(len(bufs) - 1, row) for row in range(message.shape[0])]
        return arrived

    def messages(front, back, forward, split):
        rest = back + forward
        if split:
            return [front] + ([rest] if rest else [])
        return [front + rest]

    out, bufs, pieces = None, [], []
    forward_right, forward_left, entry, earlier = [], [], 0, []
    for names, items, split, flush in steps:
        items = [send(d) for d in names] if items is None else items
        first, last = items[:1], items[1:]
        from_left = ring(messages(first, last, forward_right, split), 1)
        from_right = ring(
            messages(last, first, forward_left, split)
            if len(items) == 2
            else messages(first, last, forward_left, split),
            -1,
        )
        held = []
        for item in items:
            bufs.append(item)
            held.append([(len(bufs) - 1, row) for row in range(item.shape[0])])
        count = sum(len(rows) for rows in held)
        order = held[0] + (held[1] if len(held) == 2 else []) if held else []
        turned = held[1] + held[0] if len(held) == 2 else order
        half = len(earlier) // 2
        pieces += [(*from_left[count + j], earlier[j], 2) for j in range(half)]
        pieces += [(*from_right[count + j], earlier[half + j], 2) for j in range(half)]
        base = entry
        where = {slot: base + j for j, slot in enumerate(order)}
        for j in range(count):
            pieces += [
                (*order[j], base + j, 0),
                (*from_left[j], where[order[j]], 3),
                (*from_right[j], where[turned[j]], 1),
            ]
        earlier = [base + j for j in range(count)]
        if names == [4]:
            across = ring([items], 2)
            pieces += [(*across[j], base + j, 2) for j in range(count)]
        entry += count
        half = count // 2
        forward_right = forward_left = []
        if count:
            left_buf, right_buf = bufs[from_left[0][0]], bufs[from_right[0][0]]
            forward_right = [left_buf if left_buf.shape[0] == half else left_buf[:half]]
            if len(items) == 2:
                forward_left = [right_buf if right_buf.shape[0] == half else right_buf[:half]]
            else:
                forward_left = [right_buf[half:count]]
        if flush:
            out = place(out, pieces, dest, total[None], relay, bufs, out_shape)
            bufs, pieces = [], []
    return out


def solution(mesh):
    return jax.shard_map(
        body,
        mesh=mesh,
        in_specs=(
            P("expert", ("relay", "tensor"), None),
            P("expert", ("relay", "tensor"), None),
            P("expert", ("relay", "tensor"), None),
            P("expert", None, ("relay", "tensor"), None),
            P("expert", None, None, "tensor"),
            P(),
        ),
        out_specs=P("expert", None, "tensor", None, None),
        check_vma=False,
    )
```

```python
import functools

import jax
import jax.numpy as jnp
from jax import lax
from jax.experimental import pallas as pl
from jax.experimental.pallas import tpu as pltpu
from jax.sharding import PartitionSpec as P

ADAPTER_SCALE = 0.5
PAIR = 2


def selector(rows, cols, place):
    row = lax.broadcasted_iota(jnp.int32, (rows, cols), 0)
    col = lax.broadcasted_iota(jnp.int32, (rows, cols), 1)
    return jnp.where(col == place(row), 1.0, 0.0).astype(jnp.bfloat16)


def dot(a, b):
    return jnp.dot(a, b, preferred_element_type=jnp.float32)


def dot_t(a, b):
    return lax.dot_general(a, b, (((0,), (0,)), ((), ())), preferred_element_type=jnp.float32)


def weave_kernel(gate_hbm, up_hbm, down_hbm, woven_ref, gate_ref, up_ref, sems):
    rows, hidden = gate_ref.shape
    loads = [
        pltpu.make_async_copy(gate_hbm, gate_ref, sems.at[0]),
        pltpu.make_async_copy(up_hbm, up_ref, sems.at[1]),
        pltpu.make_async_copy(down_hbm, woven_ref.at[:, pl.ds(2 * hidden, hidden)], sems.at[2]),
    ]
    for load in loads:
        load.start()
    half = 128
    spread = selector(
        2 * half, 2 * half, lambda row: jnp.where(row < half, 2 * row, 2 * (row - half) + 1)
    )
    loads[0].wait()
    loads[1].wait()
    for block in range(hidden // half):
        src = slice(block * half, (block + 1) * half)
        dst = slice(2 * block * half, 2 * (block + 1) * half)
        both = jnp.concatenate([gate_ref[:, src], up_ref[:, src]], axis=1)
        woven_ref[:, dst] = dot(both, spread).astype(jnp.bfloat16)
    loads[2].wait()


def weave(gate, up, down):
    rows, hidden = gate.shape
    return pl.pallas_call(
        weave_kernel,
        out_shape=jax.ShapeDtypeStruct((rows, 3 * hidden), jnp.bfloat16),
        in_specs=[pl.BlockSpec(memory_space=pl.ANY)] * 3,
        out_specs=pl.BlockSpec(memory_space=pltpu.VMEM),
        scratch_shapes=[
            pltpu.VMEM((rows, hidden), jnp.bfloat16),
            pltpu.VMEM((rows, hidden), jnp.bfloat16),
            pltpu.SemaphoreType.DMA((3,)),
        ],
        compiler_params=pltpu.CompilerParams(vmem_limit_bytes=8 << 20),
        cost_estimate=pl.CostEstimate(
            flops=2 * rows * hidden * 512, bytes_accessed=2_400_000, transcendentals=0
        ),
    )(gate, up, down)


def merge_kernel(
    index_ref, tensor_ref, woven_ref, width_hbm, own_hbm, v1, v2, v3,
    self_ref, keep_ref, swap_ref, mixed_ref, plain_ref, merged_ref, width_ref, own_ref, sems,
):
    loads = [
        pltpu.make_async_copy(own_hbm, own_ref, sems.at[0]),
        pltpu.make_async_copy(width_hbm, width_ref, sems.at[1]),
    ]
    for load in loads:
        load.start()
    slabs = index_ref.shape[0]
    rows, wide = woven_ref.shape
    hidden = wide // 3
    slab_rows = rows // slabs
    rank = width_ref.shape[1]
    part = own_ref.shape[2]
    me = tensor_ref[0]
    even = selector(part, 2 * part, lambda row: 2 * row)
    odd = selector(part, 2 * part, lambda row: 2 * row + 1)
    plain_ref[...] = jnp.zeros_like(plain_ref)
    for j, v in ((1, v1), (2, v2), (3, v3), (0, own_ref)):
        if j == 0:
            loads[0].wait()
        home = lax.rem(me - j + 4, 4)
        cols = pl.ds(pl.multiple_of(home * (2 * part), 128), 2 * part)
        mixed_ref[:rank, cols] = dot(v[0], even).astype(jnp.bfloat16)
        mixed_ref[rank:, cols] = dot(v[1], odd).astype(jnp.bfloat16)
        shift = lax.rem(home, 2) * part
        pair_cols = pl.ds(pl.multiple_of(lax.div(home, 2) * (2 * part), 128), 2 * part)
        plain_ref[:, pair_cols] += dot(v[2], selector(part, 2 * part, lambda row: row + shift))
    loads[1].wait()
    both = width_ref[0:2].reshape(2 * rank, rows)
    for block in range(2 * hidden // 256):
        dst = slice(block * 256, (block + 1) * 256)
        delta = dot_t(both, mixed_ref[:, dst])
        merged_ref[:, dst] = (
            woven_ref[:, dst].astype(jnp.float32) + ADAPTER_SCALE * delta
        ).astype(jnp.bfloat16)
    delta = dot_t(width_ref[2], plain_ref[...].astype(jnp.bfloat16))
    merged_ref[:, 2 * hidden :] = (
        woven_ref[:, 2 * hidden :].astype(jnp.float32) + ADAPTER_SCALE * delta
    ).astype(jnp.bfloat16)
    bucket = swap_ref.shape[0]
    for k in range(slabs):
        index = index_ref[k]
        block = slice(k * slab_rows, (k + 1) * slab_rows)

        @pl.when(index < PAIR)
        def _():
            self_ref[index] = merged_ref[block, :]

        @pl.when((index >= PAIR) & (index < bucket))
        def _():
            keep_ref[index - PAIR] = merged_ref[block, :]

        @pl.when(index >= bucket)
        def _():
            swap_ref[index - bucket] = merged_ref[block, :]


def merge(index, tensor, woven, width, parts):
    rows, wide = woven.shape
    rank = width.shape[1]
    slab_rows = rows // index.shape[0]
    smem = pl.BlockSpec(memory_space=pltpu.SMEM)
    vmem = pl.BlockSpec(memory_space=pltpu.VMEM)

    def slots(n):
        return jax.ShapeDtypeStruct((n, slab_rows, wide), jnp.bfloat16)

    return pl.pallas_call(
        merge_kernel,
        out_shape=[slots(PAIR), slots(16 - PAIR), slots(16)],
        in_specs=[smem, smem, vmem] + [pl.BlockSpec(memory_space=pl.ANY)] * 2 + [vmem] * 3,
        out_specs=[vmem] * 3,
        scratch_shapes=[
            pltpu.VMEM((2 * rank, 2 * wide // 3), jnp.bfloat16),
            pltpu.VMEM((rank, wide // 3), jnp.float32),
            pltpu.VMEM((rows, wide), jnp.bfloat16),
            pltpu.VMEM(width.shape, jnp.bfloat16),
            pltpu.VMEM(parts[0].shape, jnp.bfloat16),
            pltpu.SemaphoreType.DMA((2,)),
        ],
        compiler_params=pltpu.CompilerParams(vmem_limit_bytes=12 << 20),
        cost_estimate=pl.CostEstimate(
            flops=2 * rows * wide * 128, bytes_accessed=4_000_000, transcendentals=0
        ),
    )(index, tensor, woven, width, *parts)


def place_kernel(pieces, count, first, dest_ref, count_ref, relay_ref, *refs):
    bufs, refs = refs[:count], refs[count if first else count + 1 :]
    out_ref, refs = refs[0], refs[1:]
    held, refs = refs[:count], refs[count:]
    load_sems, sems = refs[:2]
    groups = out_ref.shape[1]
    loads = [pltpu.make_async_copy(bufs[j], held[j], load_sems.at[j]) for j in range(count)]
    for load in loads:
        load.start()

    def copy(number):
        which, row, entry, shift = pieces[number]
        group = lax.rem(relay_ref[0] + shift, groups)
        dest = jnp.maximum(dest_ref[entry], 0)
        return pltpu.make_async_copy(
            held[which].at[row], out_ref.at[dest, group, 0], sems.at[number]
        )

    if first:
        zero_ref, zero_sems = refs[2:]

        def blank(slot):
            return pltpu.make_async_copy(zero_ref, out_ref.at[slot], zero_sems.at[slot])

        zero_ref[...] = jnp.zeros_like(zero_ref)

        @pl.loop(count_ref[0], out_ref.shape[0])
        def _(slot):
            blank(slot).start()

    ready = set()
    for number, piece in enumerate(pieces):
        if piece[0] not in ready:
            ready.add(piece[0])
            loads[piece[0]].wait()

        @pl.when(dest_ref[piece[2]] >= 0)
        def _():
            copy(number).start()

    if first:

        @pl.loop(count_ref[0], out_ref.shape[0])
        def _(slot):
            blank(slot).wait()

    for number, piece in enumerate(pieces):

        @pl.when(dest_ref[piece[2]] >= 0)
        def _():
            copy(number).wait()


def place(out, pieces, dest, total, relay, bufs, out_shape):
    smem = pl.BlockSpec(memory_space=pltpu.SMEM)
    anywhere = pl.BlockSpec(memory_space=pl.ANY)
    first = out is None
    count = len(bufs)
    pieces = sorted(pieces)
    scratch = [pltpu.VMEM(buf.shape, jnp.bfloat16) for buf in bufs]
    scratch += [pltpu.SemaphoreType.DMA((count,)), pltpu.SemaphoreType.DMA((len(pieces),))]
    if first:
        scratch += [
            pltpu.VMEM(out_shape[1:], jnp.bfloat16),
            pltpu.SemaphoreType.DMA((out_shape[0],)),
        ]
    return pl.pallas_call(
        functools.partial(place_kernel, pieces, count, first),
        out_shape=jax.ShapeDtypeStruct(out_shape, jnp.bfloat16),
        in_specs=[smem] * 3 + [anywhere] * (count if first else count + 1),
        out_specs=anywhere,
        scratch_shapes=scratch,
        input_output_aliases={} if first else {3 + count: 0},
        cost_estimate=pl.CostEstimate(
            flops=0, bytes_accessed=2 * len(pieces) * 73728, transcendentals=0
        ),
    )(dest, total, relay, *bufs, *([] if first else [out]))


def shift(value, axis, by):
    size = lax.axis_size(axis)
    return lax.ppermute(value, axis, [(i, (i + by) % size) for i in range(size)])


def body(gate, up, down, width, hidden, placement):
    owners = lax.axis_size("expert")
    chips = owners // 2
    slabs = placement.shape[1]
    me = lax.axis_index("expert").astype(jnp.int32)
    targets = lax.dynamic_index_in_dim(placement, me, 0, keepdims=False)
    iota = jnp.arange(slabs, dtype=jnp.int32)
    order = jnp.sum(
        ((targets[None, :] == targets[:, None]) & (iota[None, :] < iota[:, None])).astype(jnp.int32),
        axis=1,
    )
    offset = (targets // 2 - me // 2) % chips
    index = ((targets ^ me) & 1) * (PAIR * chips) + offset * PAIR + order
    hits = jnp.sum((placement == me).astype(jnp.int32), axis=1)
    before = jnp.sum(jnp.where(iota[None, :] < iota[:, None], hits[None, :], 0), axis=1)
    total = jnp.sum(hits)
    pair = jnp.arange(PAIR, dtype=jnp.int32)
    table = jnp.where(pair[None, :] < hits[:, None], before[:, None] + pair[None, :], -1)

    parts = [hidden[0]] + [shift(hidden[0], "tensor", k) for k in (1, 2, 3)]
    own, keep, swap = merge(
        index,
        lax.axis_index("tensor").astype(jnp.int32)[None],
        weave(gate[0], up[0], down[0]),
        jnp.swapaxes(width[0], 1, 2),
        parts,
    )
    mate = [(i, i ^ 1) for i in range(owners)]
    got = lax.ppermute(swap, "expert", mate)

    def send(d):
        rows = slice(PAIR * (d - 1), PAIR * d)
        message = jnp.concatenate([keep[rows], got[PAIR * d : PAIR * (d + 1)]], axis=0)
        return shift(message, "expert", 2 * d)

    def pair_of(d):
        return [send(d), send(chips - d)]

    near = jnp.concatenate([own, got[:PAIR]], axis=0)
    steps = [
        ([0], [near], False, False, 2),
        ([1, chips - 1], None, False, False, 1),
        ([2, chips - 2], None, False, True, 1),
        ([3, chips - 3], None, False, False, 1),
        ([4], None, True, True, 0),
    ]
    sources = jnp.stack(
        [((me - 2 * d) % owners) ^ core for names, *_ in steps for d in names for core in (0, 1)]
    )
    dest = jnp.sum(
        jnp.where(sources[:, None, None] == iota[None, :, None], table[None], 0), axis=1
    ).reshape(-1)
    relay = lax.axis_index("relay").astype(jnp.int32)[None]
    slab_rows, wide = own.shape[1:]
    out_shape = (owners * PAIR, lax.axis_size("relay"), 1, slab_rows, wide)
    def ring(parts, by):
        arrived = []
        for part in parts:
            message = part[0] if len(part) == 1 else jnp.concatenate(part, axis=0)
            bufs.append(shift(message, "relay", by))
            arrived += [(len(bufs) - 1, row) for row in range(message.shape[0])]
        return arrived

    def messages(front, back, forward, split):
        rest = back + forward
        if split:
            return [front] + ([rest] if rest else [])
        return [front + rest]

    out, bufs, pieces, entry = None, [], [], 0
    waiting = [[] for _ in range(len(steps) + 2)]
    for number, (names, items, split, flush, delay) in enumerate(steps):
        items = [send(d) for d in names] if items is None else items
        first, last = items[:1], items[1:]
        held = waiting[number]
        forward_right, forward_left = [h[0] for h in held], [h[1] for h in held]
        from_left = ring(messages(first, last, forward_right, split), 1)
        from_right = ring(
            messages(last, first, forward_left, split)
            if len(items) == 2
            else messages(first, last, forward_left, split),
            -1,
        )
        count = sum(item.shape[0] for item in items)
        row = count
        for _, _, entries in held:
            half = len(entries) // 2
            for j in range(half):
                pieces.append((*from_left[row + j], entries[j], 2))
                pieces.append((*from_right[row + j], entries[half + j], 2))
            row += half
        order = []
        for item in items:
            bufs.append(item)
            order += [(len(bufs) - 1, j) for j in range(item.shape[0])]
        half = count // 2
        turned = order[half:] + order[:half] if len(items) == 2 else order
        where = {slot: entry + j for j, slot in enumerate(order)}
        for j in range(count):
            pieces += [
                (*order[j], entry + j, 0),
                (*from_left[j], where[order[j]], 3),
                (*from_right[j], where[turned[j]], 1),
            ]
        entries = list(range(entry, entry + count))
        entry += count
        if count and delay:
            left_buf, right_buf = bufs[from_left[0][0]], bufs[from_right[0][0]]
            start = 0 if len(items) == 2 else half
            waiting[number + delay].append(
                (
                    left_buf if left_buf.shape[0] == half else left_buf[:half],
                    right_buf if right_buf.shape[0] == half else right_buf[start : start + half],
                    entries,
                )
            )
        elif count:
            across = ring([items], 2)
            pieces += [(*across[j], entries[j], 2) for j in range(count)]
        if flush:
            out = place(out, pieces, dest, total[None], relay, bufs, out_shape)
            bufs, pieces = [], []
    return out


def solution(mesh):
    return jax.shard_map(
        body,
        mesh=mesh,
        in_specs=(
            P("expert", ("relay", "tensor"), None),
            P("expert", ("relay", "tensor"), None),
            P("expert", ("relay", "tensor"), None),
            P("expert", None, ("relay", "tensor"), None),
            P("expert", None, None, "tensor"),
            P(),
        ),
        out_specs=P("expert", None, "tensor", None, None),
        check_vma=False,
    )
```

```python
import functools

import jax
import jax.numpy as jnp
from jax import lax
from jax.experimental import pallas as pl
from jax.experimental.pallas import tpu as pltpu
from jax.sharding import PartitionSpec as P

ADAPTER_SCALE = 0.5
PAIR = 2


def selector(rows, cols, place):
    row = lax.broadcasted_iota(jnp.int32, (rows, cols), 0)
    col = lax.broadcasted_iota(jnp.int32, (rows, cols), 1)
    return jnp.where(col == place(row), 1.0, 0.0).astype(jnp.bfloat16)


def dot(a, b):
    return jnp.dot(a, b, preferred_element_type=jnp.float32)


def dot_t(a, b):
    return lax.dot_general(a, b, (((0,), (0,)), ((), ())), preferred_element_type=jnp.float32)


def weave_kernel(gate_hbm, up_hbm, down_hbm, woven_ref, gate_ref, up_ref, sems):
    rows, hidden = gate_ref.shape
    loads = [
        pltpu.make_async_copy(gate_hbm, gate_ref, sems.at[0]),
        pltpu.make_async_copy(up_hbm, up_ref, sems.at[1]),
        pltpu.make_async_copy(down_hbm, woven_ref.at[:, pl.ds(2 * hidden, hidden)], sems.at[2]),
    ]
    for load in loads:
        load.start()
    half = 128
    spread = selector(
        2 * half, 2 * half, lambda row: jnp.where(row < half, 2 * row, 2 * (row - half) + 1)
    )
    loads[0].wait()
    loads[1].wait()
    for block in range(hidden // half):
        src = slice(block * half, (block + 1) * half)
        dst = slice(2 * block * half, 2 * (block + 1) * half)
        both = jnp.concatenate([gate_ref[:, src], up_ref[:, src]], axis=1)
        woven_ref[:, dst] = dot(both, spread).astype(jnp.bfloat16)
    loads[2].wait()


def weave(gate, up, down):
    rows, hidden = gate.shape
    return pl.pallas_call(
        weave_kernel,
        out_shape=jax.ShapeDtypeStruct((rows, 3 * hidden), jnp.bfloat16),
        in_specs=[pl.BlockSpec(memory_space=pl.ANY)] * 3,
        out_specs=pl.BlockSpec(memory_space=pltpu.VMEM),
        scratch_shapes=[
            pltpu.VMEM((rows, hidden), jnp.bfloat16),
            pltpu.VMEM((rows, hidden), jnp.bfloat16),
            pltpu.SemaphoreType.DMA((3,)),
        ],
        compiler_params=pltpu.CompilerParams(vmem_limit_bytes=8 << 20),
        cost_estimate=pl.CostEstimate(
            flops=2 * rows * hidden * 512, bytes_accessed=2_400_000, transcendentals=0
        ),
    )(gate, up, down)


def merge_kernel(
    index_ref, tensor_ref, woven_ref, width_hbm, own_hbm, v1, v2, v3,
    self_ref, keep_ref, swap_ref, mixed_ref, plain_ref, merged_ref, width_ref, own_ref, sems,
):
    loads = [
        pltpu.make_async_copy(own_hbm, own_ref, sems.at[0]),
        pltpu.make_async_copy(width_hbm, width_ref, sems.at[1]),
    ]
    for load in loads:
        load.start()
    slabs = index_ref.shape[0]
    rows, wide = woven_ref.shape
    hidden = wide // 3
    slab_rows = rows // slabs
    rank = width_ref.shape[1]
    part = own_ref.shape[2]
    me = tensor_ref[0]
    even = selector(part, 2 * part, lambda row: 2 * row)
    odd = selector(part, 2 * part, lambda row: 2 * row + 1)
    plain_ref[...] = jnp.zeros_like(plain_ref)
    for j, v in ((1, v1), (2, v2), (3, v3), (0, own_ref)):
        if j == 0:
            loads[0].wait()
        home = lax.rem(me - j + 4, 4)
        cols = pl.ds(pl.multiple_of(home * (2 * part), 128), 2 * part)
        mixed_ref[:rank, cols] = dot(v[0], even).astype(jnp.bfloat16)
        mixed_ref[rank:, cols] = dot(v[1], odd).astype(jnp.bfloat16)
        shift = lax.rem(home, 2) * part
        pair_cols = pl.ds(pl.multiple_of(lax.div(home, 2) * (2 * part), 128), 2 * part)
        plain_ref[:, pair_cols] += dot(v[2], selector(part, 2 * part, lambda row: row + shift))
    loads[1].wait()
    both = width_ref[0:2].reshape(2 * rank, rows)
    for block in range(2 * hidden // 256):
        dst = slice(block * 256, (block + 1) * 256)
        delta = dot_t(both, mixed_ref[:, dst])
        merged_ref[:, dst] = (
            woven_ref[:, dst].astype(jnp.float32) + ADAPTER_SCALE * delta
        ).astype(jnp.bfloat16)
    delta = dot_t(width_ref[2], plain_ref[...].astype(jnp.bfloat16))
    merged_ref[:, 2 * hidden :] = (
        woven_ref[:, 2 * hidden :].astype(jnp.float32) + ADAPTER_SCALE * delta
    ).astype(jnp.bfloat16)
    bucket = swap_ref.shape[0]
    for k in range(slabs):
        index = index_ref[k]
        block = slice(k * slab_rows, (k + 1) * slab_rows)

        @pl.when(index < PAIR)
        def _():
            self_ref[index] = merged_ref[block, :]

        @pl.when((index >= PAIR) & (index < bucket))
        def _():
            keep_ref[index - PAIR] = merged_ref[block, :]

        @pl.when(index >= bucket)
        def _():
            swap_ref[index - bucket] = merged_ref[block, :]


def merge(index, tensor, woven, width, parts):
    rows, wide = woven.shape
    rank = width.shape[1]
    slab_rows = rows // index.shape[0]
    smem = pl.BlockSpec(memory_space=pltpu.SMEM)
    vmem = pl.BlockSpec(memory_space=pltpu.VMEM)

    def slots(n):
        return jax.ShapeDtypeStruct((n, slab_rows, wide), jnp.bfloat16)

    return pl.pallas_call(
        merge_kernel,
        out_shape=[slots(PAIR), slots(16 - PAIR), slots(16)],
        in_specs=[smem, smem, vmem] + [pl.BlockSpec(memory_space=pl.ANY)] * 2 + [vmem] * 3,
        out_specs=[vmem] * 3,
        scratch_shapes=[
            pltpu.VMEM((2 * rank, 2 * wide // 3), jnp.bfloat16),
            pltpu.VMEM((rank, wide // 3), jnp.float32),
            pltpu.VMEM((rows, wide), jnp.bfloat16),
            pltpu.VMEM(width.shape, jnp.bfloat16),
            pltpu.VMEM(parts[0].shape, jnp.bfloat16),
            pltpu.SemaphoreType.DMA((2,)),
        ],
        compiler_params=pltpu.CompilerParams(vmem_limit_bytes=12 << 20),
        cost_estimate=pl.CostEstimate(
            flops=2 * rows * wide * 128, bytes_accessed=4_000_000, transcendentals=0
        ),
    )(index, tensor, woven, width, *parts)


def place_kernel(pieces, count, first, dest_ref, count_ref, relay_ref, *refs):
    bufs, refs = refs[:count], refs[count if first else count + 1 :]
    out_ref, refs = refs[0], refs[1:]
    held, refs = refs[:count], refs[count:]
    load_sems, sems = refs[:2]
    groups = out_ref.shape[1]
    loads = [pltpu.make_async_copy(bufs[j], held[j], load_sems.at[j]) for j in range(count)]
    for load in loads:
        load.start()

    def copy(number):
        which, row, entry, shift = pieces[number]
        group = lax.rem(relay_ref[0] + shift, groups)
        dest = jnp.maximum(dest_ref[entry], 0)
        return pltpu.make_async_copy(
            held[which].at[row], out_ref.at[dest, group, 0], sems.at[number]
        )

    if first:
        zero_ref, zero_sems = refs[2:]

        def blank(slot):
            return pltpu.make_async_copy(zero_ref, out_ref.at[slot], zero_sems.at[slot])

        zero_ref[...] = jnp.zeros_like(zero_ref)

        @pl.loop(count_ref[0], out_ref.shape[0])
        def _(slot):
            blank(slot).start()

    ready = set()
    for number, piece in enumerate(pieces):
        if piece[0] not in ready:
            ready.add(piece[0])
            loads[piece[0]].wait()

        @pl.when(dest_ref[piece[2]] >= 0)
        def _():
            copy(number).start()

    if first:

        @pl.loop(count_ref[0], out_ref.shape[0])
        def _(slot):
            blank(slot).wait()

    for number, piece in enumerate(pieces):

        @pl.when(dest_ref[piece[2]] >= 0)
        def _():
            copy(number).wait()


def place(out, pieces, dest, total, relay, bufs, out_shape):
    smem = pl.BlockSpec(memory_space=pltpu.SMEM)
    anywhere = pl.BlockSpec(memory_space=pl.ANY)
    first = out is None
    count = len(bufs)
    pieces = sorted(pieces)
    scratch = [pltpu.VMEM(buf.shape, jnp.bfloat16) for buf in bufs]
    scratch += [pltpu.SemaphoreType.DMA((count,)), pltpu.SemaphoreType.DMA((len(pieces),))]
    if first:
        scratch += [
            pltpu.VMEM(out_shape[1:], jnp.bfloat16),
            pltpu.SemaphoreType.DMA((out_shape[0],)),
        ]
    return pl.pallas_call(
        functools.partial(place_kernel, pieces, count, first),
        out_shape=jax.ShapeDtypeStruct(out_shape, jnp.bfloat16),
        in_specs=[smem] * 3 + [anywhere] * (count if first else count + 1),
        out_specs=anywhere,
        scratch_shapes=scratch,
        input_output_aliases={} if first else {3 + count: 0},
        cost_estimate=pl.CostEstimate(
            flops=0, bytes_accessed=2 * len(pieces) * 73728, transcendentals=0
        ),
    )(dest, total, relay, *bufs, *([] if first else [out]))


def shift(value, axis, by):
    size = lax.axis_size(axis)
    return lax.ppermute(value, axis, [(i, (i + by) % size) for i in range(size)])


def body(gate, up, down, width, hidden, placement):
    owners = lax.axis_size("expert")
    chips = owners // 2
    slabs = placement.shape[1]
    me = lax.axis_index("expert").astype(jnp.int32)
    targets = lax.dynamic_index_in_dim(placement, me, 0, keepdims=False)
    iota = jnp.arange(slabs, dtype=jnp.int32)
    order = jnp.sum(
        ((targets[None, :] == targets[:, None]) & (iota[None, :] < iota[:, None])).astype(jnp.int32),
        axis=1,
    )
    offset = (targets // 2 - me // 2) % chips
    index = ((targets ^ me) & 1) * (PAIR * chips) + offset * PAIR + order
    hits = jnp.sum((placement == me).astype(jnp.int32), axis=1)
    before = jnp.sum(jnp.where(iota[None, :] < iota[:, None], hits[None, :], 0), axis=1)
    total = jnp.sum(hits)
    pair = jnp.arange(PAIR, dtype=jnp.int32)
    table = jnp.where(pair[None, :] < hits[:, None], before[:, None] + pair[None, :], -1)

    parts = [hidden[0]] + [shift(hidden[0], "tensor", k) for k in (1, 2, 3)]
    own, keep, swap = merge(
        index,
        lax.axis_index("tensor").astype(jnp.int32)[None],
        weave(gate[0], up[0], down[0]),
        jnp.swapaxes(width[0], 1, 2),
        parts,
    )
    mate = [(i, i ^ 1) for i in range(owners)]
    got = lax.ppermute(swap, "expert", mate)

    def send(d):
        rows = slice(PAIR * (d - 1), PAIR * d)
        message = jnp.concatenate([keep[rows], got[PAIR * d : PAIR * (d + 1)]], axis=0)
        return shift(message, "expert", 2 * d)

    def pair_of(d):
        return [send(d), send(chips - d)]

    near = jnp.concatenate([own, got[:PAIR]], axis=0)
    steps = [
        ([0], [near], False, False, 2),
        ([1, chips - 1], None, False, False, 1),
        ([2, chips - 2], None, False, True, 1),
        ([3, chips - 3], None, False, False, 1),
        ([4], None, False, True, 0),
    ]
    sources = jnp.stack(
        [((me - 2 * d) % owners) ^ core for names, *_ in steps for d in names for core in (0, 1)]
    )
    dest = jnp.sum(
        jnp.where(sources[:, None, None] == iota[None, :, None], table[None], 0), axis=1
    ).reshape(-1)
    relay = lax.axis_index("relay").astype(jnp.int32)[None]
    slab_rows, wide = own.shape[1:]
    out_shape = (owners * PAIR, lax.axis_size("relay"), 1, slab_rows, wide)
    def ring(parts, by):
        arrived = []
        for part in parts:
            message = part[0] if len(part) == 1 else jnp.concatenate(part, axis=0)
            bufs.append(shift(message, "relay", by))
            arrived += [(len(bufs) - 1, row) for row in range(message.shape[0])]
        return arrived

    def messages(front, back, forward, split):
        rest = back + forward
        if split:
            return [front] + ([rest] if rest else [])
        return [front + rest]

    out, bufs, pieces, entry = None, [], [], 0
    waiting = [[] for _ in range(len(steps) + 2)]
    for number, (names, items, split, flush, delay) in enumerate(steps):
        items = [send(d) for d in names] if items is None else items
        first, last = items[:1], items[1:]
        held = waiting[number]
        forward_right, forward_left = [h[0] for h in held], [h[1] for h in held]
        from_left = ring(messages(first, last, forward_right, split), 1)
        from_right = ring(
            messages(last, first, forward_left, split)
            if len(items) == 2
            else messages(first, last, forward_left, split),
            -1,
        )
        count = sum(item.shape[0] for item in items)
        row = count
        for _, _, entries in held:
            half = len(entries) // 2
            for j in range(half):
                pieces.append((*from_left[row + j], entries[j], 2))
                pieces.append((*from_right[row + j], entries[half + j], 2))
            row += half
        order = []
        for item in items:
            bufs.append(item)
            order += [(len(bufs) - 1, j) for j in range(item.shape[0])]
        half = count // 2
        turned = order[half:] + order[:half] if len(items) == 2 else order
        where = {slot: entry + j for j, slot in enumerate(order)}
        for j in range(count):
            pieces += [
                (*order[j], entry + j, 0),
                (*from_left[j], where[order[j]], 3),
                (*from_right[j], where[turned[j]], 1),
            ]
        entries = list(range(entry, entry + count))
        entry += count
        if count and delay:
            left_buf, right_buf = bufs[from_left[0][0]], bufs[from_right[0][0]]
            start = 0 if len(items) == 2 else half
            waiting[number + delay].append(
                (
                    left_buf if left_buf.shape[0] == half else left_buf[:half],
                    right_buf if right_buf.shape[0] == half else right_buf[start : start + half],
                    entries,
                )
            )
        elif count:
            across = ring([items], 2)
            pieces += [(*across[j], entries[j], 2) for j in range(count)]
        if flush:
            out = place(out, pieces, dest, total[None], relay, bufs, out_shape)
            bufs, pieces = [], []
    return out


def solution(mesh):
    return jax.shard_map(
        body,
        mesh=mesh,
        in_specs=(
            P("expert", ("relay", "tensor"), None),
            P("expert", ("relay", "tensor"), None),
            P("expert", ("relay", "tensor"), None),
            P("expert", None, ("relay", "tensor"), None),
            P("expert", None, None, "tensor"),
            P(),
        ),
        out_specs=P("expert", None, "tensor", None, None),
        check_vma=False,
    )
```
